32 devices in a mesh: expert: 4 (over y, core), tensor: 2 (over x), dp: 4 (over z).
Axes of the slice: x: 2, y: 2, z: 4, core: 2. Of those that a mesh axis runs over, the one named last changes fastest.
Arguments:
- tokens: bfloat16 [2048, 4096], P(('expert', 'dp'), 'tensor'), may hold values from -6 to 6
- routes: int32 [2048, 2], P(('expert', 'dp')), may hold values from 0 to 3, all different within a row; in each aligned block of 128 rows (0 to 127, 128 to 255, ...) at most 80 rows name the same one
- gate_prob: float32 [2048, 2], P(('expert', 'dp')), may hold values from 0.05 to 1
- token_count: int32 [16], P(('expert', 'dp')), may hold values from 1 to 128, 1536 in all
- gate_weight: bfloat16 [4, 4096, 1536], P(None, ('expert', 'dp'), 'tensor'), may hold values from -0.09375 to 0.09375
- up_weight: bfloat16 [4, 4096, 1536], P(None, ('expert', 'dp'), 'tensor'), may hold values from -0.09375 to 0.09375
- down_weight: bfloat16 [4, 4096, 1536], P(None, ('expert', 'dp'), 'tensor'), may hold values from -0.15625 to 0.15625
Outputs:
- mixed: bfloat16 [2048, 4096], P(('expert', 'dp'), 'tensor')
The draws below stay inside these ranges and needn't reach their ends.
Inputs may be any that keep to these rules, and one draw needn't show every extreme that they name: `routes`: each row names 2 different experts; among the rows of one group (aligned blocks of 128 rows) no expert is named by more than 80 rows. `token_count`: rows of a group at or past its count are padding.
All inputs are finite; a program needn't handle non-finite values.
Results may differ from the reference program's by a relative error of at most 0.012.
Values may be sent and summed in bfloat16 or wider, within the bound.
No kernel may reach another device: no remote copies, remote signals or barrier semaphores. Data moves between devices by JAX's collectives and lax.ppermute only.
A program may use at most 64 MiB of HBM per device.

```python
import math
import jax
import jax.numpy as jnp
import numpy as np
from jax import lax

D = 4096
FF = 1536
TOPW = 2
TOK_DEV = 128
EXPERTS = 4
GROUPS = 16
TOKENS = 2048
CAP = 80
N_TENSOR = 2


def shard_levels(rng, extent, pieces, smallest, largest):
    def one(dim, shards_of):
        heights = jax.random.uniform(jax.random.fold_in(jax.random.fold_in(rng, 6), dim), (shards_of,), jnp.float32, smallest / len(pieces), largest / len(pieces))
        return jnp.repeat(jnp.exp(heights), extent[dim] // shards_of).reshape((-1,) + (1,) * (len(extent) - dim - 1))

    level = one(*pieces[0])
    for cut in pieces[1:]:
        level = level * one(*cut)
    return level


def split_up(count, total, most, lean):
    portions = [(1 << 20) // math.isqrt(standing ** lean) + 1 for standing in range(2, count + 1)]
    surplus, counts = total - most - (count - 1), [1] * (count - 1)
    while surplus > 0:
        movable = [i for i in range(count - 1) if counts[i] < most]
        whole, budget = sum([portions[i] for i in movable]), surplus
        for i in movable:
            extra = min(most - counts[i], max(1, budget * portions[i] // whole), surplus)
            counts[i] = counts[i] + extra
            surplus = surplus - extra
    return np.array([most] + counts)


def uneven_parts(rng, count, total, limit, slope):
    if count == 2:
        one = jax.random.randint(rng, (), max(1, total - limit), min(limit, total - 1) + 1)
        return jnp.stack([one, total - one])
    sizes = jnp.asarray(split_up(count, total, limit, slope), jnp.int32)
    pairs = (count - 1) // 2
    donor, sink = sizes[1:1 + 2 * pairs:2], sizes[2:2 + 2 * pairs:2]
    slack = jnp.minimum(donor - 1, limit - sink)
    moved = jax.random.randint(jax.random.fold_in(rng, 1), (pairs,), 0, 1 << 20) % (slack + 1)
    sizes = sizes.at[1:1 + 2 * pairs:2].set(donor - moved).at[2:2 + 2 * pairs:2].set(sink + moved)
    return sizes[jax.random.permutation(jax.random.fold_in(rng, 2), count)]


def assign_block(own_key, own, number, rows, count, top, limit, skew):
    order = jax.random.permutation(own_key, count)
    packed, ordinary = load_shares(count, rows * top, limit, skew, True), load_shares(count, rows * top, limit, skew, False)
    places = jnp.arange(count)

    def named(tallies, rotation):
        used = int((tallies > 0).sum())
        fixed = max(1, used // 4)
        passed = fixed + (places - fixed + rotation * (used - fixed)) % max(1, count - fixed)
        return jnp.zeros((count,), jnp.int32).at[order[jnp.where(places < fixed, places, passed)]].set(jnp.asarray(tallies, jnp.int32))

    tallies = jnp.where(number % 4 == 0, named(packed, number // 4), named(ordinary, number - number // 4 - 1))
    mixed = jax.random.permutation(jax.random.fold_in(own, 3), count)
    source_of, receiver = mixed[0:count // 2 * 2:2], mixed[1:count // 2 * 2:2]
    margin = jnp.minimum(tallies[source_of] - 1, limit - tallies[receiver]) // 2
    margin = jnp.where((source_of == order[0]) | (receiver == order[0]) | (tallies[receiver] == 0), 0, jnp.maximum(margin, 0))
    passed = jax.random.randint(jax.random.fold_in(own, 4), (count // 2,), 0, 1 << 20) % (margin + 1)
    tallies = tallies.at[source_of].add(-passed).at[receiver].add(passed)
    labels = jnp.searchsorted(jnp.cumsum(tallies), jnp.arange(rows * top), side="right").astype(jnp.int32)
    grid = labels.reshape(top, rows).T
    grid = grid[jax.random.permutation(jax.random.fold_in(own, 1), rows)]
    rotation = jax.random.randint(jax.random.fold_in(own, 2), (rows, 1), 0, top)
    return jnp.take_along_axis(grid, (jnp.arange(top)[None, :] + rotation) % top, axis=1)


def load_shares(number_of, total, limit, slope, full):
    loads = [(1 << 20) // math.isqrt(grade ** slope) + 1 for grade in range(1, number_of + 1)]
    largest = limit if full else min(limit, max(-(-total // number_of), total * loads[0] // sum(loads)))
    least = 1 if total - largest >= number_of - 1 else 0
    given, spare = [largest] + [least] * (number_of - 1), total - largest - least * (number_of - 1)
    while spare > 0:
        movable = [i for i in range(1, number_of) if given[i] < largest] or [i for i in range(1, number_of) if given[i] < limit]
        whole, left = sum([loads[i] for i in movable]), spare
        for i in movable:
            addition = min(limit - given[i], max(1, left * loads[i] // whole), spare)
            given[i] = given[i] + addition
            spare = spare - addition
    return np.array(given)


def noise(stream_key, extent, deviation, bound, split=(), held_as=jnp.bfloat16):
    factor_of = shard_levels(stream_key, extent, split, -0.22, 0.18) if split else 1.0
    entries = jax.random.normal(stream_key, extent, jnp.float32) * deviation * factor_of
    return jnp.minimum(jnp.maximum(entries, -bound), bound).astype(held_as)


def setup_inputs(seed: int = 0) -> dict:
    splits = jax.random.split(jax.random.key(seed), 8)
    tokens = noise(splits[0], (TOKENS, D), 1.0, 6.0, ((0, 16), (1, 2)))
    routes_keys = jax.random.split(jax.random.fold_in(splits[1], 1), TOKENS // TOK_DEV)
    routes_turns = jax.random.permutation(jax.random.fold_in(splits[1], 3), TOKENS // TOK_DEV)
    routes = jax.vmap(lambda own, number: assign_block(jax.random.fold_in(splits[1], 2), own, number, TOK_DEV, EXPERTS, TOPW, CAP, 1))(routes_keys, routes_turns).reshape((TOKENS, TOPW))
    gate_prob = jnp.clip(jnp.exp(math.log(1.0) - 2.9957323 * jax.random.uniform(splits[2], (TOKENS, TOPW), jnp.float32) ** shard_levels(splits[2], (TOKENS, TOPW), ((0, 16),), -0.2, 0.2)), 0.05, 1.0)
    token_count = uneven_parts(splits[3], GROUPS, 3 * TOKENS // 4, TOK_DEV, 1).astype(jnp.int32)
    gate_weight = noise(splits[4], (EXPERTS, D, FF), D ** -0.5, 0.09375, ((1, 16), (2, 2)))
    up_weight = noise(splits[5], (EXPERTS, D, FF), D ** -0.5, 0.09375, ((1, 16), (2, 2)))
    down_weight = noise(splits[6], (EXPERTS, D, FF), FF ** -0.5, 0.15625, ((1, 16), (2, 2)))
    return {"tokens": tokens, "routes": routes, "gate_prob": gate_prob, "token_count": token_count, "gate_weight": gate_weight, "up_weight": up_weight, "down_weight": down_weight}


def reference(tokens, routes, gate_prob, token_count, gate_weight, up_weight, down_weight):
    groups = token_count.shape[0]
    tok_dev = tokens.shape[0] // groups
    experts = gate_weight.shape[0]
    top_slots = routes.shape[1]
    model_width = tokens.shape[1]
    hidden_units = gate_weight.shape[2]
    capacity = CAP
    positions = jnp.arange(tok_dev).astype(jnp.int32)
    live_rows = positions[None, :] < token_count[:, None]
    live_pair = jnp.repeat(live_rows, top_slots, axis=1)
    route_flat = routes.reshape(groups, tok_dev * top_slots)
    expert_ids = jnp.arange(experts).astype(jnp.int32)
    one_hot = ((route_flat[:, :, None] == expert_ids[None, None, :]) & live_pair[:, :, None]).astype(jnp.int32)
    pair_rank = jnp.sum((jnp.cumsum(one_hot, axis=1) - one_hot) * one_hot, axis=2).astype(jnp.int32)
    group_ids = jnp.arange(groups).astype(jnp.int32)
    global_tok = (group_ids[:, None] * tok_dev + jnp.repeat(positions, top_slots)[None, :]).astype(jnp.int32)
    slot_expert = jnp.where(live_pair, route_flat, experts).astype(jnp.int32)
    group_index = jnp.broadcast_to(group_ids[:, None], route_flat.shape)
    index_table = jnp.zeros((experts, groups, capacity), jnp.int32)
    weight_table = jnp.zeros((experts, groups, capacity), jnp.float32)
    index_table = index_table.at[slot_expert, group_index, pair_rank].set(global_tok, mode="drop")
    weight_table = weight_table.at[slot_expert, group_index, pair_rank].set(gate_prob.reshape(groups, -1).astype(jnp.float32), mode="drop")
    quarter_width = hidden_units // N_TENSOR

    def one_expert(running, inputs):
        index_rows, weight_rows, w_gate, w_up, w_down = inputs
        flat_index = index_rows.reshape(-1)
        gathered = tokens[flat_index]
        gate_proj = jnp.dot(gathered, w_gate, preferred_element_type=jnp.float32)
        up_proj = jnp.dot(gathered, w_up, preferred_element_type=jnp.float32)
        hidden = (jax.nn.silu(gate_proj) * up_proj).astype(jnp.bfloat16)
        partial_value = jnp.zeros((gathered.shape[0], model_width), jnp.float32)
        for quarter_index in range(N_TENSOR):
            low = quarter_index * quarter_width
            term_piece = lax.dot_general(hidden[:, low:low + quarter_width], w_down[:, low:low + quarter_width], (((1,), (1,)), ((), ())), preferred_element_type=jnp.float32)
            rounded = lax.optimization_barrier(term_piece.astype(jnp.bfloat16))
            partial_value = partial_value + rounded.astype(jnp.float32)
        result = lax.optimization_barrier(partial_value.astype(jnp.bfloat16)).astype(jnp.float32)
        running = running.at[flat_index].add(weight_rows.reshape(-1)[:, None] * result)
        return running, jnp.zeros((), jnp.float32)

    start_total = jnp.zeros((tokens.shape[0], model_width), jnp.float32)
    running, unused = lax.scan(one_expert, start_total, (index_table, weight_table, gate_weight, up_weight, down_weight))
    return running.astype(jnp.bfloat16)
```

```python
import functools

import jax
import jax.numpy as jnp
from jax import lax
from jax.experimental import pallas as pl
from jax.experimental.pallas import tpu as pltpu
from jax.sharding import PartitionSpec as P

BF = jnp.bfloat16
F32 = jnp.float32
VMEM_BYTES = 48 * 1024 * 1024


def gathered_plan(tokens, routes, gate_prob, token_count, gate_weight, up_weight, down_weight):
    experts = gate_weight.shape[0]
    stored_rows = gate_weight.shape[1]
    hidden_share = gate_weight.shape[2]
    tok_rows, top_slots = routes.shape
    capacity = min(tok_rows, tok_rows * top_slots * 5 // (4 * experts))
    expert_count = lax.axis_size("expert")
    replica_count = lax.axis_size("dp")
    model_width = stored_rows * expert_count * replica_count

    def relay(weight):
        arrived = lax.all_to_all(weight, "expert", split_axis=0, concat_axis=1, tiled=True)
        blocks = arrived.reshape(1, expert_count, 1, stored_rows, hidden_share)
        return lax.all_gather(blocks, "dp", axis=2, tiled=True).reshape(model_width, hidden_share)

    w_gate, w_up, w_down = relay(gate_weight), relay(up_weight), relay(down_weight)
    positions = jnp.arange(tok_rows)
    live_rows = positions < token_count[0]
    live_pair = jnp.repeat(live_rows, top_slots)
    route_flat = routes.reshape(-1)
    expert_ids = jnp.arange(experts)
    one_hot = ((route_flat[:, None] == expert_ids[None, :]) & live_pair[:, None]).astype(jnp.int32)
    pair_rank = jnp.sum((jnp.cumsum(one_hot, axis=0) - one_hot) * one_hot, axis=1)
    slot_of_pair = jnp.where(live_pair, route_flat * capacity + pair_rank, -1)
    slot_ids = jnp.arange(experts * capacity)
    assign_pair = (slot_ids[:, None] == slot_of_pair[None, :]).astype(BF)
    assign_slots = assign_pair.reshape(experts * capacity, tok_rows, top_slots)
    assign_bf16 = jnp.sum(assign_slots.astype(F32), axis=2).astype(BF)
    outgoing = jnp.dot(assign_bf16, tokens, preferred_element_type=F32).astype(BF)
    incoming = lax.all_to_all(
        outgoing.reshape(experts, capacity, tokens.shape[1]), "expert", split_axis=0, concat_axis=0, tiled=True
    )
    feature_piece = lax.all_gather(incoming, "tensor", axis=2, tiled=True)
    flat_piece = feature_piece.reshape(-1, feature_piece.shape[2])
    gate_proj = jnp.dot(flat_piece, w_gate, preferred_element_type=F32)
    up_proj = jnp.dot(flat_piece, w_up, preferred_element_type=F32)
    hidden = (jax.nn.silu(gate_proj) * up_proj).astype(BF)
    partial_value = lax.dot_general(hidden, w_down, (((1,), (1,)), ((), ())), preferred_element_type=F32)
    expert_out = lax.psum_scatter(partial_value.astype(BF), "tensor", scatter_dimension=1, tiled=True)
    returned = lax.all_to_all(
        expert_out.reshape(experts, capacity, -1), "expert", split_axis=0, concat_axis=0, tiled=True
    )
    returned_rows = returned.reshape(experts * capacity, -1)
    picked = jnp.einsum("cts,cd->std", assign_slots, returned_rows, preferred_element_type=F32)
    mixed = jnp.sum(gate_prob.T[:, :, None] * picked, axis=0)
    return mixed.astype(BF)


def group_of(where_ref, block, n_dp):
    z = lax.rem(where_ref[2] - block + n_dp, n_dp)
    return (where_ref[0] * 2 + where_ref[1]) * n_dp + z


def columns_of(where_ref, meta_ref, blocks, n_dp):
    parts = [meta_ref[group_of(where_ref, b, n_dp)] for b in blocks]
    return jnp.concatenate(parts, axis=0)


def send_order_kernel(where_ref, tokens_ref, *out_refs):
    n_dp = len(out_refs)
    width = tokens_ref.shape[1] // (2 * n_dp)
    core, z = where_ref[1], where_ref[2]
    for k, out in enumerate(out_refs):
        target = lax.rem(z + k, n_dp)
        for j in range(2):
            slot = (lax.rem(core + j, 2) * n_dp + target) * width
            out[:, j * width : (j + 1) * width] = tokens_ref[:, pl.ds(pl.multiple_of(slot, width), width)]


def place_kernel(where_ref, *refs):
    in_refs, out_ref = refs[:-1], refs[-1]
    n_dp = len(in_refs)
    width = out_ref.shape[1] // (2 * n_dp)
    core, z = where_ref[1], where_ref[2]
    for k, piece in enumerate(in_refs):
        source = lax.rem(z + k, n_dp)
        for j in range(2):
            slot = (lax.rem(core + j, 2) * n_dp + source) * width
            out_ref[:, pl.ds(pl.multiple_of(slot, width), width)] = piece[:, j * width : (j + 1) * width]


def gate_up_kernel(n_dp, where_ref, meta_ref, own_ref, far_ref, w0, w1, w2, w3, *out_refs):
    same = where_ref[3] == 1
    rows = own_ref.shape[1]
    experts, width = w0.shape[0], w0.shape[1]
    own = own_ref[...].reshape(n_dp * rows, 2 * width)
    far = far_ref[...].reshape(n_dp * rows, 2 * width)
    near_x = jnp.where(same, own, far)
    away_x = jnp.where(same, far, own)
    meta = columns_of(where_ref, meta_ref, range(n_dp), n_dp)
    slots = [None, None]
    for e in range(experts):
        part = jnp.dot(near_x[:, :width], w0[e], preferred_element_type=F32)
        part += jnp.dot(near_x[:, width:], w1[e], preferred_element_type=F32)
        part += jnp.dot(away_x[:, :width], w2[e], preferred_element_type=F32)
        part += jnp.dot(away_x[:, width:], w3[e], preferred_element_type=F32)
        for s in range(2):
            held = jnp.zeros_like(part) if e == 0 else slots[s]
            slots[s] = jnp.where(meta[:, s : s + 1] == float(e), part, held)
    for k, out in enumerate(out_refs):
        for s in range(2):
            out[s] = slots[s][k * rows : (k + 1) * rows].astype(BF)


def down_kernel(n_dp, where_ref, meta_ref, *refs):
    h_refs = refs[:n_dp]
    w_refs = refs[n_dp : n_dp + 4]
    near_out, away_out = refs[n_dp + 4 :]
    same = where_ref[3] == 1
    rows = h_refs[0].shape[1]
    experts, width = w_refs[0].shape[0], w_refs[0].shape[1]
    meta = columns_of(where_ref, meta_ref, range(n_dp), n_dp)
    h0 = jnp.concatenate([h[0] for h in h_refs], axis=0)
    h1 = jnp.concatenate([h[1] for h in h_refs], axis=0)
    total = [None] * 4
    for e in range(experts):
        first, second = meta[:, 0:1] == float(e), meta[:, 1:2] == float(e)
        h_e = jnp.where(first, h0, jnp.where(second, h1, jnp.zeros_like(h1)))
        scale = jnp.where(first, meta[:, 2:3], jnp.where(second, meta[:, 3:4], 0.0))
        for j in range(4):
            term = scale * lax.dot_general(h_e, w_refs[j][e], (((1,), (1,)), ((), ())), preferred_element_type=F32)
            total[j] = term if e == 0 else total[j] + term
    held = [t.astype(BF).reshape(n_dp, rows, width) for t in total]
    for j in range(2):
        cols = slice(j * width, (j + 1) * width)
        near_out[:, :, cols] = jnp.where(same, held[j], held[j + 2])
        away_out[:, :, cols] = jnp.where(same, held[j + 2], held[j])


SMEM = pl.BlockSpec(memory_space=pltpu.SMEM)
WHOLE = pl.BlockSpec(memory_space=pltpu.VMEM)
PARAMS = pltpu.CompilerParams(vmem_limit_bytes=VMEM_BYTES)


def stationary_plan(tokens, routes, gate_prob, token_count, gate_weight, up_weight, down_weight):
    experts, width, share = gate_weight.shape
    half = share // 2
    rows = tokens.shape[0]
    n_dp = lax.axis_size("dp")
    place = lax.axis_index("expert")
    y, core, x, z = place // 2, place % 2, lax.axis_index("tensor"), lax.axis_index("dp")
    same = (x == y).astype(jnp.int32)
    near = jnp.stack([y, core, z, same]).astype(jnp.int32)
    away = jnp.stack([1 - y, core, z, same]).astype(jnp.int32)

    def swap_y(v):
        return lax.ppermute(v, "expert", [(0, 2), (2, 0), (1, 3), (3, 1)])

    def swap_core(v):
        return lax.ppermute(v, "expert", [(0, 1), (1, 0), (2, 3), (3, 2)])

    def swap_x(v):
        return lax.ppermute(v, "tensor", [(0, 1), (1, 0)])

    def swap_xy(v):
        pairs = [(e * 2 + t, ((e + 2) % 4) * 2 + 1 - t) for e in range(4) for t in range(2)]
        return lax.ppermute(v, ("expert", "tensor"), pairs)

    def shift(v, k):
        return lax.ppermute(v, "dp", [(i, (i + k) % n_dp) for i in range(n_dp)])

    def cut(weight, which):
        return lax.dynamic_slice_in_dim(weight, which * half, half, axis=2)

    gu_send = jnp.concatenate([cut(gate_weight, 1 - y), cut(up_weight, 1 - y)], axis=2)
    gu_y = swap_y(gu_send)
    gu_keep = jnp.concatenate([cut(gate_weight, y), cut(up_weight, y)], axis=2)
    gu_core = swap_core(gu_keep)

    live = jnp.arange(rows)[:, None] < token_count[0]
    meta = jnp.concatenate([jnp.where(live, routes, -1).astype(F32), gate_prob], axis=1)
    metas = lax.all_gather(meta.T, ("expert", "dp"), axis=0).transpose(0, 2, 1)

    send = pl.pallas_call(
        send_order_kernel,
        out_shape=[jax.ShapeDtypeStruct((rows, 2 * width), BF)] * n_dp,
        in_specs=[SMEM, WHOLE],
        out_specs=[WHOLE] * n_dp,
        compiler_params=PARAMS,
    )(near, tokens)
    own = jnp.stack([send[0]] + [shift(send[k], k) for k in range(1, n_dp)])
    own_x = swap_x(own)
    own_y = swap_y(own)
    own_xy = swap_xy(own)
    gu_yc = swap_core(gu_y)

    down_send = cut(down_weight, 1 - y)
    down_send, _ = lax.optimization_barrier((down_send, gu_y))
    down_y = swap_y(down_send)
    down_keep = cut(down_weight, y)
    down_core = swap_core(down_keep)
    down_yc = swap_core(down_y)

    tile = 256
    steps = (2 * half) // tile

    def gate_up(where, mine, other):
        w_spec = pl.BlockSpec((experts, width, tile), lambda n: (0, 0, n))
        return pl.pallas_call(
            functools.partial(gate_up_kernel, n_dp),
            grid=(steps,),
            out_shape=[jax.ShapeDtypeStruct((2, rows, 2 * half), BF)] * n_dp,
            in_specs=[
                SMEM,
                pl.BlockSpec(metas.shape, lambda n: (0, 0, 0)),
                pl.BlockSpec(mine.shape, lambda n: (0, 0, 0)),
                pl.BlockSpec(other.shape, lambda n: (0, 0, 0)),
            ]
            + [w_spec] * 4,
            out_specs=[pl.BlockSpec((2, rows, tile), lambda n: (0, 0, n))] * n_dp,
            compiler_params=PARAMS,
        )(where, metas, mine, other, gu_keep, gu_core, gu_y, gu_yc)

    def ring_sum(parts):
        run = parts[1]
        for k in range(2, n_dp + 1):
            got = shift(run, 1).astype(F32)
            total = parts[k % n_dp].astype(F32) + got
            run = total if k == n_dp else total.astype(BF)
        return run

    def hidden_of(total):
        gate, up = total[..., :half], total[..., half:]
        return (jax.nn.silu(gate) * up).astype(BF)

    def down(where, hidden):
        return pl.pallas_call(
            functools.partial(down_kernel, n_dp),
            out_shape=[jax.ShapeDtypeStruct((n_dp, rows, 2 * width), BF)] * 2,
            in_specs=[SMEM] + [WHOLE] * (n_dp + 5),
            out_specs=[WHOLE] * 2,
            compiler_params=PARAMS,
        )(where, metas, *hidden, down_keep, down_core, down_y, down_yc)

    def gather_dp(v):
        return [v] + [shift(v, k) for k in range(1, n_dp)]

    parts_near = gate_up(near, own, own_x)
    parts_away = gate_up(away, own_y, own_xy)
    hidden_near = gather_dp(hidden_of(ring_sum(parts_near)))
    hidden_away = gather_dp(hidden_of(ring_sum(parts_away)))
    near_mine, near_x = down(near, hidden_near)
    away_y, away_xy = down(away, hidden_away)
    total = near_mine.astype(F32) + swap_x(near_x).astype(F32)
    total = total + swap_y(away_y).astype(F32) + swap_xy(away_xy).astype(F32)
    total = total.astype(BF)
    back = [total[0]] + [shift(total[k], -k) for k in range(1, n_dp)]
    return pl.pallas_call(
        place_kernel,
        out_shape=jax.ShapeDtypeStruct(tokens.shape, BF),
        in_specs=[SMEM] + [WHOLE] * n_dp,
        out_specs=WHOLE,
        compiler_params=PARAMS,
    )(near, *back)


def solution(mesh):
    in_specs = (
        P(("expert", "dp"), "tensor"),
        P(("expert", "dp"), None),
        P(("expert", "dp"), None),
        P(("expert", "dp")),
        P(None, ("expert", "dp"), "tensor"),
        P(None, ("expert", "dp"), "tensor"),
        P(None, ("expert", "dp"), "tensor"),
    )
    out_specs = P(("expert", "dp"), "tensor")
    plan = stationary_plan if mesh.shape["expert"] == 4 and mesh.shape["tensor"] == 2 else gathered_plan
    return jax.shard_map(plan, mesh=mesh, in_specs=in_specs, out_specs=out_specs, check_vma=False)
```

```python
import functools

import jax
import jax.numpy as jnp
from jax import lax
from jax.experimental import pallas as pl
from jax.experimental.pallas import tpu as pltpu
from jax.sharding import PartitionSpec as P

BF = jnp.bfloat16
F32 = jnp.float32
VMEM_BYTES = 48 * 1024 * 1024


def gathered_plan(tokens, routes, gate_prob, token_count, gate_weight, up_weight, down_weight):
    experts = gate_weight.shape[0]
    stored_rows = gate_weight.shape[1]
    hidden_share = gate_weight.shape[2]
    tok_rows, top_slots = routes.shape
    capacity = min(tok_rows, tok_rows * top_slots * 5 // (4 * experts))
    expert_count = lax.axis_size("expert")
    replica_count = lax.axis_size("dp")
    model_width = stored_rows * expert_count * replica_count

    def relay(weight):
        arrived = lax.all_to_all(weight, "expert", split_axis=0, concat_axis=1, tiled=True)
        blocks = arrived.reshape(1, expert_count, 1, stored_rows, hidden_share)
        return lax.all_gather(blocks, "dp", axis=2, tiled=True).reshape(model_width, hidden_share)

    w_gate, w_up, w_down = relay(gate_weight), relay(up_weight), relay(down_weight)
    positions = jnp.arange(tok_rows)
    live_rows = positions < token_count[0]
    live_pair = jnp.repeat(live_rows, top_slots)
    route_flat = routes.reshape(-1)
    expert_ids = jnp.arange(experts)
    one_hot = ((route_flat[:, None] == expert_ids[None, :]) & live_pair[:, None]).astype(jnp.int32)
    pair_rank = jnp.sum((jnp.cumsum(one_hot, axis=0) - one_hot) * one_hot, axis=1)
    slot_of_pair = jnp.where(live_pair, route_flat * capacity + pair_rank, -1)
    slot_ids = jnp.arange(experts * capacity)
    assign_pair = (slot_ids[:, None] == slot_of_pair[None, :]).astype(BF)
    assign_slots = assign_pair.reshape(experts * capacity, tok_rows, top_slots)
    assign_bf16 = jnp.sum(assign_slots.astype(F32), axis=2).astype(BF)
    outgoing = jnp.dot(assign_bf16, tokens, preferred_element_type=F32).astype(BF)
    incoming = lax.all_to_all(
        outgoing.reshape(experts, capacity, tokens.shape[1]), "expert", split_axis=0, concat_axis=0, tiled=True
    )
    feature_piece = lax.all_gather(incoming, "tensor", axis=2, tiled=True)
    flat_piece = feature_piece.reshape(-1, feature_piece.shape[2])
    gate_proj = jnp.dot(flat_piece, w_gate, preferred_element_type=F32)
    up_proj = jnp.dot(flat_piece, w_up, preferred_element_type=F32)
    hidden = (jax.nn.silu(gate_proj) * up_proj).astype(BF)
    partial_value = lax.dot_general(hidden, w_down, (((1,), (1,)), ((), ())), preferred_element_type=F32)
    expert_out = lax.psum_scatter(partial_value.astype(BF), "tensor", scatter_dimension=1, tiled=True)
    returned = lax.all_to_all(
        expert_out.reshape(experts, capacity, -1), "expert", split_axis=0, concat_axis=0, tiled=True
    )
    returned_rows = returned.reshape(experts * capacity, -1)
    picked = jnp.einsum("cts,cd->std", assign_slots, returned_rows, preferred_element_type=F32)
    mixed = jnp.sum(gate_prob.T[:, :, None] * picked, axis=0)
    return mixed.astype(BF)


META_ROWS = 16
UNIT = 128


def split_in_three(value):
    high = value.astype(BF)
    rest = value - high.astype(F32)
    middle = rest.astype(BF)
    return high, middle, (rest - middle.astype(F32)).astype(BF)


def columns_of(token_refs, rows):
    held = jnp.concatenate([t[rows:, :rows].astype(F32).T for t in token_refs], axis=0)
    prob = [held[:, 2 + s : 3 + s] + held[:, 4 + s : 5 + s] + held[:, 6 + s : 7 + s] for s in range(2)]
    return held[:, 0:1], held[:, 1:2], prob[0], prob[1]


def send_order_kernel(where_ref, tokens_ref, route_ref, prob_ref, *out_refs):
    n_dp = len(out_refs)
    rows = tokens_ref.shape[0]
    width = tokens_ref.shape[1] // (2 * n_dp)
    core, z = where_ref[1], where_ref[2]
    meta = [route_ref[...].astype(BF), *split_in_three(prob_ref[...])]
    for k, out in enumerate(out_refs):
        target = lax.rem(z + k, n_dp)
        for j in range(2):
            slot = (lax.rem(core + j, 2) * n_dp + target) * width
            out[:rows, j * width : (j + 1) * width] = tokens_ref[:, pl.ds(pl.multiple_of(slot, width), width)]
        filler = jnp.zeros((META_ROWS - 8, rows), F32)
        block = jnp.concatenate([m.astype(F32) for m in meta] + [filler], axis=0).astype(BF)
        out[rows:, :] = jnp.zeros((META_ROWS, 2 * width), BF)
        out[rows:, :rows] = block


def place_kernel(where_ref, *refs):
    in_refs, out_ref = refs[:-1], refs[-1]
    n_dp = len(in_refs)
    width = out_ref.shape[1] // (2 * n_dp)
    core, z = where_ref[1], where_ref[2]
    for k, piece in enumerate(in_refs):
        source = lax.rem(z + k, n_dp)
        for j in range(2):
            slot = (lax.rem(core + j, 2) * n_dp + source) * width
            out_ref[:, pl.ds(pl.multiple_of(slot, width), width)] = piece[:, j * width : (j + 1) * width]


def gate_up_kernel(n_dp, where_ref, *refs):
    own_refs, far_refs = refs[:n_dp], refs[n_dp : 2 * n_dp]
    w_refs = refs[2 * n_dp : 2 * n_dp + 4]
    out_refs = refs[2 * n_dp + 4 :]
    same = where_ref[3] == 1
    rows = own_refs[0].shape[0] - META_ROWS
    blocks, experts, width, tile = w_refs[0].shape
    own = jnp.concatenate([r[:rows] for r in own_refs], axis=0)
    far = jnp.concatenate([r[:rows] for r in far_refs], axis=0)
    near_x = jnp.where(same, own, far)
    away_x = jnp.where(same, far, own)
    pieces = (near_x[:, :width], near_x[:, width:], away_x[:, :width], away_x[:, width:])
    route = columns_of(own_refs, rows)[:2]
    for b in range(blocks):
        slots = [None, None]
        for e in range(experts):
            part = sum(jnp.dot(p, w[b, e], preferred_element_type=F32) for p, w in zip(pieces, w_refs))
            for s in range(2):
                held = jnp.zeros_like(part) if e == 0 else slots[s]
                slots[s] = jnp.where(route[s] == float(e), part, held)
        for k, out in enumerate(out_refs):
            for s in range(2):
                out[s, :, b * tile : (b + 1) * tile] = slots[s][k * rows : (k + 1) * rows].astype(BF)


def hidden_kernel(n_spans, *refs):
    mine, got, out_ref = refs[:n_spans], refs[n_spans : 2 * n_spans], refs[-1]
    unit, at = UNIT, 0
    for a, b in zip(mine, got):
        for n in range(a.shape[-1] // (2 * unit)):
            gate_cols = slice(2 * n * unit, (2 * n + 1) * unit)
            up_cols = slice((2 * n + 1) * unit, (2 * n + 2) * unit)
            for s in range(2):
                gate = a[s, :, gate_cols].astype(F32) + b[s, :, gate_cols].astype(F32)
                up = a[s, :, up_cols].astype(F32) + b[s, :, up_cols].astype(F32)
                out_ref[s, :, at : at + unit] = (gate / (1.0 + jnp.exp(-gate)) * up).astype(BF)
            at += unit


def down_kernel(n_blocks, where_ref, *refs):
    token_refs, h_refs = refs[:n_blocks], refs[n_blocks : 2 * n_blocks]
    w_refs = refs[2 * n_blocks : 2 * n_blocks + 4]
    near_out, away_out = refs[2 * n_blocks + 4 :]
    same = where_ref[3] == 1
    rows = h_refs[0].shape[1]
    experts, width = w_refs[0].shape[0], w_refs[0].shape[1]
    route0, route1, prob0, prob1 = columns_of(token_refs, rows)
    h0 = jnp.concatenate([h[0] for h in h_refs], axis=0)
    h1 = jnp.concatenate([h[1] for h in h_refs], axis=0)
    total = [None] * 4
    for e in range(experts):
        first, second = route0 == float(e), route1 == float(e)
        h_e = jnp.where(first, h0, jnp.where(second, h1, jnp.zeros_like(h1)))
        scale = jnp.where(first, prob0, jnp.where(second, prob1, 0.0))
        for j in range(4):
            term = scale * lax.dot_general(h_e, w_refs[j][e], (((1,), (1,)), ((), ())), preferred_element_type=F32)
            total[j] = term if e == 0 else total[j] + term
    held = [t.astype(BF).reshape(n_blocks, rows, width) for t in total]
    for j in range(2):
        cols = slice(j * width, (j + 1) * width)
        near_out[:, :, cols] = jnp.where(same, held[j], held[j + 2])
        away_out[:, :, cols] = jnp.where(same, held[j + 2], held[j])


SMEM = pl.BlockSpec(memory_space=pltpu.SMEM)
WHOLE = pl.BlockSpec(memory_space=pltpu.VMEM)
PARAMS = pltpu.CompilerParams(vmem_limit_bytes=VMEM_BYTES)
LIGHT = pl.CostEstimate(flops=1, bytes_accessed=1, transcendentals=0)


def stationary_plan(tokens, routes, gate_prob, token_count, gate_weight, up_weight, down_weight):
    experts, width, share = gate_weight.shape
    half = share // 2
    rows = tokens.shape[0]
    n_dp = lax.axis_size("dp")
    place = lax.axis_index("expert")
    y, core, x, z = place // 2, place % 2, lax.axis_index("tensor"), lax.axis_index("dp")
    same = (x == y).astype(jnp.int32)
    where = jnp.stack([y, core, z, (x == y).astype(jnp.int32)]).astype(jnp.int32)

    def swap_y(v):
        return lax.ppermute(v, "expert", [(0, 2), (2, 0), (1, 3), (3, 1)])

    def swap_core(v):
        return lax.ppermute(v, "expert", [(0, 1), (1, 0), (2, 3), (3, 2)])

    def swap_x(v):
        return lax.ppermute(v, "tensor", [(0, 1), (1, 0)])

    def swap_xy(v):
        pairs = [(e * 2 + t, ((e + 2) % 4) * 2 + 1 - t) for e in range(4) for t in range(2)]
        return lax.ppermute(v, ("expert", "tensor"), pairs)

    def shift(v, k):
        return lax.ppermute(v, "dp", [(i, (i + k) % n_dp) for i in range(n_dp)])

    def cut(weight, which):
        return lax.dynamic_slice_in_dim(weight, which * half, half, axis=2)

    live = jnp.arange(rows)[None, :] < token_count[0]
    slots = jnp.where(live, routes.T, -1).astype(F32)

    send = pl.pallas_call(
        send_order_kernel,
        out_shape=[jax.ShapeDtypeStruct((rows + META_ROWS, 2 * width), BF)] * n_dp,
        in_specs=[SMEM] + [WHOLE] * 3,
        out_specs=[WHOLE] * n_dp,
        compiler_params=PARAMS,
        cost_estimate=LIGHT,
    )(where, tokens, slots, gate_prob.T)
    own = jnp.stack([send[0]] + [shift(send[k], k) for k in range(1, n_dp)])

    unit = UNIT

    def gate_up_blocks(which, first, count):
        def block(n):
            start = which * half + n * unit
            return jnp.concatenate(
                [lax.dynamic_slice_in_dim(w, start, unit, axis=2) for w in (gate_weight, up_weight)], axis=2
            )

        return jnp.stack([block(n) for n in range(first, first + count)])

    blocks = half // unit
    spans = [(0, 1), (1, blocks - 1)]
    gu_send = [gate_up_blocks(1 - y, *span) for span in spans]
    gu_send[0], _ = lax.optimization_barrier((gu_send[0], send[0]))
    gu_keep = [gate_up_blocks(y, *span) for span in spans]
    gu_core = [swap_core(v) for v in gu_keep]
    gu_y = [swap_y(gu_send[0])]
    own, gu_y[0], *gu_core = lax.optimization_barrier((own, gu_y[0], *gu_core))

    own_x, own_y = swap_x(own), swap_y(own)
    gu_yc = [swap_core(gu_y[0])]
    own_x, own_y, gu_yc[0], gu_send[1] = lax.optimization_barrier((own_x, own_y, gu_yc[0], gu_send[1]))
    own_xy = swap_x(own_y)
    gu_y.append(swap_y(gu_send[1]))

    def gate_up(span, mine, other):
        weights = (gu_keep[span], gu_core[span], gu_y[span], gu_yc[span])
        columns = weights[0].shape[0] * 2 * unit
        held = [pl.BlockSpec((None,) + mine.shape[1:], lambda n, k=k: (k, 0, 0)) for k in range(n_dp)]
        outs = pl.pallas_call(
            functools.partial(gate_up_kernel, n_dp),
            grid=(1,),
            out_shape=[jax.ShapeDtypeStruct((2, rows, columns), BF)] * n_dp,
            in_specs=[SMEM] + held * 2 + [WHOLE] * 4,
            out_specs=[WHOLE] * n_dp,
            compiler_params=PARAMS,
            cost_estimate=LIGHT,
        )(where, *[mine] * n_dp, *[other] * n_dp, *weights)
        return list(outs)

    def ring_step(parts, run, k):
        return (parts[k].astype(F32) + shift(run, 1).astype(F32)).astype(BF)

    def hidden_of(parts, gots):
        return pl.pallas_call(
            functools.partial(hidden_kernel, len(parts)),
            out_shape=jax.ShapeDtypeStruct((2, rows, half), BF),
            in_specs=[WHOLE] * (2 * len(parts)),
            out_specs=WHOLE,
            compiler_params=PARAMS,
            cost_estimate=LIGHT,
        )(*[p[0] for p in parts], *gots)

    near0 = gate_up(0, own, own_x)
    run_near0 = near0[1]
    for k in range(2, n_dp):
        run_near0 = ring_step(near0, run_near0, k)
    own_xy, run_near0 = lax.optimization_barrier((own_xy, run_near0))
    got_near0 = shift(run_near0, 1)
    away0 = gate_up(0, own_y, own_xy)
    run_away0 = ring_step(away0, away0[1], 2)
    gu_y[1], run_away0, got_near0 = lax.optimization_barrier((gu_y[1], run_away0, got_near0))
    gu_yc.append(swap_core(gu_y[1]))
    for k in range(3, n_dp):
        run_away0 = ring_step(away0, run_away0, k)
    got_away0 = shift(run_away0, 1)
    near1, away1 = gate_up(1, own, own_x), gate_up(1, own_y, own_xy)
    run_near1, run_away1 = near1[1], away1[1]
    for k in range(2, n_dp):
        run_away1 = ring_step(away1, run_away1, k)
        run_near1 = ring_step(near1, run_near1, k)
    hidden_away = hidden_of([away0, away1], [got_away0, shift(run_away1, 1)])
    hidden_near = hidden_of([near0, near1], [got_near0, shift(run_near1, 1)])

    down_send, _ = lax.optimization_barrier((cut(down_weight, 1 - y), gu_y[1]))
    down_y = swap_y(down_send)
    down_keep = cut(down_weight, y)
    down_core = swap_core(down_keep)
    down_yc = swap_core(down_y)

    def down(mine, hidden):
        held = [pl.BlockSpec((None,) + mine.shape[1:], lambda n, k=k: (k, 0, 0)) for k in range(n_dp)]
        return pl.pallas_call(
            functools.partial(down_kernel, n_dp),
            grid=(1,),
            out_shape=[jax.ShapeDtypeStruct((n_dp, rows, 2 * width), BF)] * 2,
            in_specs=[SMEM] + held + [WHOLE] * (n_dp + 4),
            out_specs=[WHOLE] * 2,
            compiler_params=PARAMS,
            cost_estimate=LIGHT,
        )(where, *[mine] * n_dp, *hidden, down_keep, down_core, down_y, down_yc)

    def gather_dp(v):
        return [v] + [shift(v, k) for k in range(1, n_dp)]

    hidden_away = gather_dp(hidden_away)
    hidden_near, *hidden_away = lax.optimization_barrier((hidden_near, *hidden_away))
    hidden_near = gather_dp(hidden_near)
    away_y, away_xy = down(own_y, hidden_away)
    near_mine, near_x = down(own, hidden_near)
    total = near_mine.astype(F32) + swap_y(away_y).astype(F32) + swap_xy(away_xy).astype(F32)
    total = (total + swap_x(near_x).astype(F32)).astype(BF)
    back = [total[0]] + [shift(total[k], -k) for k in range(1, n_dp)]
    return pl.pallas_call(
        place_kernel,
        out_shape=jax.ShapeDtypeStruct(tokens.shape, BF),
        in_specs=[SMEM] + [WHOLE] * n_dp,
        out_specs=WHOLE,
        compiler_params=PARAMS,
        cost_estimate=LIGHT,
    )(where, *back)


def solution(mesh):
    in_specs = (
        P(("expert", "dp"), "tensor"),
        P(("expert", "dp"), None),
        P(("expert", "dp"), None),
        P(("expert", "dp")),
        P(None, ("expert", "dp"), "tensor"),
        P(None, ("expert", "dp"), "tensor"),
        P(None, ("expert", "dp"), "tensor"),
    )
    out_specs = P(("expert", "dp"), "tensor")
    plan = stationary_plan if mesh.shape["expert"] == 4 and mesh.shape["tensor"] == 2 else gathered_plan
    return jax.shard_map(plan, mesh=mesh, in_specs=in_specs, out_specs=out_specs, check_vma=False)
```

```python
import functools

import jax
import jax.numpy as jnp
from jax import lax
from jax.experimental import pallas as pl
from jax.experimental.pallas import tpu as pltpu
from jax.sharding import PartitionSpec as P

BF = jnp.bfloat16
F32 = jnp.float32
VMEM_BYTES = 48 * 1024 * 1024


def gathered_plan(tokens, routes, gate_prob, token_count, gate_weight, up_weight, down_weight):
    experts = gate_weight.shape[0]
    stored_rows = gate_weight.shape[1]
    hidden_share = gate_weight.shape[2]
    tok_rows, top_slots = routes.shape
    capacity = min(tok_rows, tok_rows * top_slots * 5 // (4 * experts))
    expert_count = lax.axis_size("expert")
    replica_count = lax.axis_size("dp")
    model_width = stored_rows * expert_count * replica_count

    def relay(weight):
        arrived = lax.all_to_all(weight, "expert", split_axis=0, concat_axis=1, tiled=True)
        blocks = arrived.reshape(1, expert_count, 1, stored_rows, hidden_share)
        return lax.all_gather(blocks, "dp", axis=2, tiled=True).reshape(model_width, hidden_share)

    w_gate, w_up, w_down = relay(gate_weight), relay(up_weight), relay(down_weight)
    positions = jnp.arange(tok_rows)
    live_rows = positions < token_count[0]
    live_pair = jnp.repeat(live_rows, top_slots)
    route_flat = routes.reshape(-1)
    expert_ids = jnp.arange(experts)
    one_hot = ((route_flat[:, None] == expert_ids[None, :]) & live_pair[:, None]).astype(jnp.int32)
    pair_rank = jnp.sum((jnp.cumsum(one_hot, axis=0) - one_hot) * one_hot, axis=1)
    slot_of_pair = jnp.where(live_pair, route_flat * capacity + pair_rank, -1)
    slot_ids = jnp.arange(experts * capacity)
    assign_pair = (slot_ids[:, None] == slot_of_pair[None, :]).astype(BF)
    assign_slots = assign_pair.reshape(experts * capacity, tok_rows, top_slots)
    assign_bf16 = jnp.sum(assign_slots.astype(F32), axis=2).astype(BF)
    outgoing = jnp.dot(assign_bf16, tokens, preferred_element_type=F32).astype(BF)
    incoming = lax.all_to_all(
        outgoing.reshape(experts, capacity, tokens.shape[1]), "expert", split_axis=0, concat_axis=0, tiled=True
    )
    feature_piece = lax.all_gather(incoming, "tensor", axis=2, tiled=True)
    flat_piece = feature_piece.reshape(-1, feature_piece.shape[2])
    gate_proj = jnp.dot(flat_piece, w_gate, preferred_element_type=F32)
    up_proj = jnp.dot(flat_piece, w_up, preferred_element_type=F32)
    hidden = (jax.nn.silu(gate_proj) * up_proj).astype(BF)
    partial_value = lax.dot_general(hidden, w_down, (((1,), (1,)), ((), ())), preferred_element_type=F32)
    expert_out = lax.psum_scatter(partial_value.astype(BF), "tensor", scatter_dimension=1, tiled=True)
    returned = lax.all_to_all(
        expert_out.reshape(experts, capacity, -1), "expert", split_axis=0, concat_axis=0, tiled=True
    )
    returned_rows = returned.reshape(experts * capacity, -1)
    picked = jnp.einsum("cts,cd->std", assign_slots, returned_rows, preferred_element_type=F32)
    mixed = jnp.sum(gate_prob.T[:, :, None] * picked, axis=0)
    return mixed.astype(BF)


META_ROWS = 16
UNIT = 128


def split_in_three(value):
    high = value.astype(BF)
    rest = value - high.astype(F32)
    middle = rest.astype(BF)
    return high, middle, (rest - middle.astype(F32)).astype(BF)


def columns_of(token_refs, rows):
    held = jnp.concatenate([t[rows:, :rows].astype(F32).T for t in token_refs], axis=0)
    prob = [held[:, 2 + s : 3 + s] + held[:, 4 + s : 5 + s] + held[:, 6 + s : 7 + s] for s in range(2)]
    return held[:, 0:1], held[:, 1:2], prob[0], prob[1]


def send_order_kernel(where_ref, tokens_ref, route_ref, prob_ref, *out_refs):
    n_dp = len(out_refs)
    rows = tokens_ref.shape[0]
    width = tokens_ref.shape[1] // (2 * n_dp)
    core, z = where_ref[1], where_ref[2]
    meta = [route_ref[...].astype(BF), *split_in_three(prob_ref[...])]
    for k, out in enumerate(out_refs):
        target = lax.rem(z + k, n_dp)
        for j in range(2):
            slot = (lax.rem(core + j, 2) * n_dp + target) * width
            out[:rows, j * width : (j + 1) * width] = tokens_ref[:, pl.ds(pl.multiple_of(slot, width), width)]
        filler = jnp.zeros((META_ROWS - 8, rows), F32)
        block = jnp.concatenate([m.astype(F32) for m in meta] + [filler], axis=0).astype(BF)
        out[rows:, :] = jnp.zeros((META_ROWS, 2 * width), BF)
        out[rows:, :rows] = block


def place_kernel(where_ref, *refs):
    in_refs, out_ref = refs[:-1], refs[-1]
    n_dp = len(in_refs)
    width = out_ref.shape[1] // (2 * n_dp)
    core, z = where_ref[1], where_ref[2]
    for k, piece in enumerate(in_refs):
        source = lax.rem(z + k, n_dp)
        for j in range(2):
            slot = (lax.rem(core + j, 2) * n_dp + source) * width
            out_ref[:, pl.ds(pl.multiple_of(slot, width), width)] = piece[:, j * width : (j + 1) * width]


def gate_up_kernel(n, where_ref, *refs):
    own_refs, far_refs, out_refs = refs[:n], refs[n : 2 * n], refs[-n:]
    w_refs = refs[2 * n : -n]
    same = where_ref[3] == 1
    rows = own_refs[0].shape[0] - META_ROWS
    own = jnp.concatenate([r[:rows] for r in own_refs], axis=0)
    far = jnp.concatenate([r[:rows] for r in far_refs], axis=0)
    near_x = jnp.where(same, own, far)
    away_x = jnp.where(same, far, own)
    route = columns_of(own_refs, rows)[:2]
    for b in range(len(w_refs) // 6):
        gate, up, gate_core, up_core, far_w, far_core = w_refs[6 * b : 6 * b + 6]
        experts, width, unit = gate.shape
        slots = [None, None]
        for e in range(experts):
            mine = jnp.concatenate([gate[e], up[e]], axis=1)
            cores = jnp.concatenate([gate_core[e], up_core[e]], axis=1)
            part = jnp.dot(near_x[:, :width], mine, preferred_element_type=F32)
            part += jnp.dot(near_x[:, width:], cores, preferred_element_type=F32)
            part += jnp.dot(away_x[:, :width], far_w[e], preferred_element_type=F32)
            part += jnp.dot(away_x[:, width:], far_core[e], preferred_element_type=F32)
            for s in range(2):
                held = jnp.zeros_like(part) if e == 0 else slots[s]
                slots[s] = jnp.where(route[s] == float(e), part, held)
        for k, out in enumerate(out_refs):
            for s in range(2):
                out[s, :, 2 * b * unit : 2 * (b + 1) * unit] = slots[s][k * rows : (k + 1) * rows].astype(BF)


def hidden_kernel(n_spans, *refs):
    mine, got, out_ref = refs[:n_spans], refs[n_spans : 2 * n_spans], refs[-1]
    unit, at = UNIT, 0
    for a, b in zip(mine, got):
        for n in range(a.shape[-1] // (2 * unit)):
            gate_cols = slice(2 * n * unit, (2 * n + 1) * unit)
            up_cols = slice((2 * n + 1) * unit, (2 * n + 2) * unit)
            for s in range(2):
                gate = a[s, :, gate_cols].astype(F32) + b[s, :, gate_cols].astype(F32)
                up = a[s, :, up_cols].astype(F32) + b[s, :, up_cols].astype(F32)
                out_ref[s, :, at : at + unit] = (gate / (1.0 + jnp.exp(-gate)) * up).astype(BF)
            at += unit


def down_kernel(n, n_parts, first, where_ref, *refs):
    token_refs = refs[:n]
    h_refs = refs[n : n * (1 + n_parts)]
    w_refs = refs[n * (1 + n_parts) : n * (1 + n_parts) + 4]
    rest = refs[n * (1 + n_parts) + 4 :]
    same = where_ref[3] == 1
    rows = h_refs[0].shape[1]
    experts, width = w_refs[0].shape[0], w_refs[0].shape[1]
    route0, route1, prob0, prob1 = columns_of(token_refs, rows)
    hidden = [
        jnp.concatenate(
            [jnp.concatenate([h_refs[p * n + i][s] for p in range(n_parts)], axis=1) for i in range(n)], axis=0
        )
        for s in range(2)
    ]
    total = [None] * 4
    if not first:
        total = [jnp.concatenate([rest[i][:, j * width : (j + 1) * width] for i in range(n)], axis=0) for j in range(4)]
    for e in range(experts):
        one, two = route0 == float(e), route1 == float(e)
        h_e = jnp.where(one, hidden[0], jnp.where(two, hidden[1], jnp.zeros_like(hidden[1])))
        scale = jnp.where(one, prob0, jnp.where(two, prob1, 0.0))
        for j in range(4):
            term = scale * lax.dot_general(h_e, w_refs[j][e], (((1,), (1,)), ((), ())), preferred_element_type=F32)
            total[j] = term if total[j] is None else total[j] + term
    if first:
        for i in range(n):
            for j in range(4):
                rest[i][:, j * width : (j + 1) * width] = total[j][i * rows : (i + 1) * rows]
        return
    near_out, away_out = rest[n:]
    held = [t.astype(BF).reshape(n, rows, width) for t in total]
    for j in range(2):
        cols = slice(j * width, (j + 1) * width)
        near_out[:, :, cols] = jnp.where(same, held[j], held[j + 2])
        away_out[:, :, cols] = jnp.where(same, held[j + 2], held[j])


SMEM = pl.BlockSpec(memory_space=pltpu.SMEM)
WHOLE = pl.BlockSpec(memory_space=pltpu.VMEM)
PARAMS = pltpu.CompilerParams(vmem_limit_bytes=VMEM_BYTES)
LIGHT = pl.CostEstimate(flops=1, bytes_accessed=1, transcendentals=0)


def stationary_plan(tokens, routes, gate_prob, token_count, gate_weight, up_weight, down_weight):
    experts, width, share = gate_weight.shape
    rows = tokens.shape[0]
    n_dp = lax.axis_size("dp")
    place = lax.axis_index("expert")
    y, core, x, z = place // 2, place % 2, lax.axis_index("tensor"), lax.axis_index("dp")
    same = (x == y).astype(jnp.int32)
    where = jnp.stack([y, core, z, (x == y).astype(jnp.int32)]).astype(jnp.int32)

    def swap_y(v):
        return lax.ppermute(v, "expert", [(0, 2), (2, 0), (1, 3), (3, 1)])

    def swap_core(v):
        return lax.ppermute(v, "expert", [(0, 1), (1, 0), (2, 3), (3, 2)])

    def swap_x(v):
        return lax.ppermute(v, "tensor", [(0, 1), (1, 0)])

    def shift(v, k):
        return lax.ppermute(v, "dp", [(i, (i + k) % n_dp) for i in range(n_dp)])

    live = jnp.arange(rows)[None, :] < token_count[0]
    slots = jnp.where(live, routes.T, -1).astype(F32)

    send = pl.pallas_call(
        send_order_kernel,
        out_shape=[jax.ShapeDtypeStruct((rows + META_ROWS, 2 * width), BF)] * n_dp,
        in_specs=[SMEM] + [WHOLE] * 3,
        out_specs=[WHOLE] * n_dp,
        compiler_params=PARAMS,
        cost_estimate=LIGHT,
    )(where, tokens, slots, gate_prob.T)
    def cross_x(v, k):
        pairs = [(t * n_dp + i, (1 - t) * n_dp + (i + k) % n_dp) for t in range(2) for i in range(n_dp)]
        return lax.ppermute(v, ("tensor", "dp"), pairs)

    gate_core, up_core = swap_core(gate_weight), swap_core(up_weight)
    gate_core, up_core, *send = lax.optimization_barrier((gate_core, up_core, *send))
    own = [send[0]] + [shift(send[k], k) for k in range(1, n_dp)]
    stacked = swap_x(jnp.stack(own))
    far = [stacked[k] for k in range(n_dp)]

    blocks = share // UNIT

    def block(weights, n):
        return jnp.concatenate([w[:, :, n * UNIT : (n + 1) * UNIT] for w in weights], axis=2)

    def gate_up(units, over_y, over_y_core):
        def call(which):
            n = len(which)
            weights, w_specs = [], []
            for i in units:
                weights += [gate_weight, up_weight, gate_core, up_core]
                w_specs += [pl.BlockSpec((experts, width, UNIT), lambda _, i=i: (0, 0, i))] * 4
                for v in (over_y, over_y_core):
                    weights.append(v)
                    w_specs.append(pl.BlockSpec((None,) + v.shape[1:], lambda _, at=i - units[0]: (at, 0, 0, 0)))
            return pl.pallas_call(
                functools.partial(gate_up_kernel, n),
                grid=(1,),
                out_shape=[jax.ShapeDtypeStruct((2, rows, 2 * len(units) * UNIT), BF)] * n,
                in_specs=[SMEM] + [WHOLE] * (2 * n) + w_specs,
                out_specs=[WHOLE] * n,
                compiler_params=PARAMS,
                cost_estimate=LIGHT,
            )(where, *[own[k] for k in which], *[far[k] for k in which], *weights)

        (sent,) = call([1])
        kept = call([0] + list(range(2, n_dp)))
        return [kept[0], sent, *kept[1:]]

    def ring_step(parts, run, k):
        return (parts[k].astype(F32) + shift(run, 1).astype(F32)).astype(BF)

    def hidden_of(parts, gots):
        columns = sum(p[0].shape[2] for p in parts) // 2
        return pl.pallas_call(
            functools.partial(hidden_kernel, len(parts)),
            out_shape=jax.ShapeDtypeStruct((2, rows, columns), BF),
            in_specs=[WHOLE] * (2 * len(parts)),
            out_specs=WHOLE,
            compiler_params=PARAMS,
            cost_estimate=LIGHT,
        )(*[p[0] for p in parts], *gots)

    def ring_dp(v):
        held = [v]
        for _ in range(1, n_dp):
            held.append(shift(held[-1], 1))
        return held

    def gather_dp(v):
        return [v] + [shift(v, k) for k in range(1, n_dp)]

    bar = lax.optimization_barrier
    given = (gate_weight, up_weight)

    def pair(n):
        return jnp.stack([block(given, n), block(given, n + 1)])

    y01 = swap_y(pair(0))
    own, far, y01, *given = bar((own, far, y01, *given))

    yc01 = swap_core(y01)
    y23 = swap_y(pair(2))
    parts0 = gate_up([0, 1], y01, yc01)
    run0 = ring_step(parts0, parts0[1], 2)
    run0 = ring_step(parts0, run0, 3)
    y23, run0, *given = bar((y23, run0, *given))

    yc23 = swap_core(y23)
    y45 = swap_y(pair(4))
    got0 = shift(run0, 1)
    parts1 = gate_up([2, 3], y23, yc23)
    run1 = ring_step(parts1, parts1[1], 2)
    hidden0 = gather_dp(hidden_of([parts0], [got0]))
    run1 = ring_step(parts1, run1, 3)
    y45, run1, down_from, *hidden0 = bar((y45, run1, down_weight, *hidden0))

    yc45 = swap_core(y45)
    down_y = swap_y(down_from)
    got1 = shift(run1, 1)
    parts2 = gate_up([4, 5], y45, yc45)
    run2 = ring_step(parts2, parts2[1], 2)
    hidden1 = ring_dp(hidden_of([parts1], [got1]))
    run2 = ring_step(parts2, run2, 3)
    got2 = shift(run2, 1)
    got2, down_y, down_from, *hidden1 = bar((got2, down_y, down_from, *hidden1))
    down_core, down_yc = swap_core(down_from), swap_core(down_y)
    hidden2 = hidden_of([parts2], [got2])
    hidden2 = gather_dp(hidden2)
    hidden2[1], down_core, down_yc = bar((hidden2[1], down_core, down_yc))

    down_weights = (down_weight, down_core, down_y, down_yc)
    late = 2 * UNIT
    sums = pl.pallas_call(
        functools.partial(down_kernel, n_dp, 2, True),
        grid=(1,),
        out_shape=[jax.ShapeDtypeStruct((rows, 4 * width), F32)] * n_dp,
        in_specs=[SMEM]
        + [WHOLE] * (3 * n_dp)
        + [pl.BlockSpec((experts, width, share - late), lambda _: (0, 0, 0))] * 4,
        out_specs=[WHOLE] * n_dp,
        compiler_params=PARAMS,
        cost_estimate=pl.CostEstimate(flops=6_000_000_000, bytes_accessed=1, transcendentals=0),
    )(where, *own, *hidden0, *hidden1, *down_weights)

    hidden2[1], hidden2[2], hidden2[3], *sums = bar((hidden2[1], hidden2[2], hidden2[3], *sums))

    def down(which):
        n = len(which)
        last = pl.BlockSpec((experts, width, late), lambda _: (0, 0, share // late - 1))
        return pl.pallas_call(
            functools.partial(down_kernel, n, 1, False),
            grid=(1,),
            out_shape=[jax.ShapeDtypeStruct((n, rows, 2 * width), BF)] * 2,
            in_specs=[SMEM] + [WHOLE] * (2 * n) + [last] * 4 + [WHOLE] * n,
            out_specs=[WHOLE] * 2,
            compiler_params=PARAMS,
            cost_estimate=LIGHT,
        )(where, *[own[k] for k in which], *[hidden2[k] for k in which], *down_weights, *[sums[k] for k in which])

    back = [None] * n_dp
    order = list(range(2, n_dp)) + [1, 0]
    for which in (order[: n_dp // 2], order[n_dp // 2 :]):
        mine, other = down(which)
        total = (mine.astype(F32) + swap_x(other).astype(F32)).astype(BF)
        for i, k in enumerate(which):
            back[k] = total[i] if k == 0 else shift(total[i], -k)
    return pl.pallas_call(
        place_kernel,
        out_shape=jax.ShapeDtypeStruct(tokens.shape, BF),
        in_specs=[SMEM] + [WHOLE] * n_dp,
        out_specs=WHOLE,
        compiler_params=PARAMS,
        cost_estimate=LIGHT,
    )(where, *back)


def solution(mesh):
    in_specs = (
        P(("expert", "dp"), "tensor"),
        P(("expert", "dp"), None),
        P(("expert", "dp"), None),
        P(("expert", "dp")),
        P(None, ("expert", "dp"), "tensor"),
        P(None, ("expert", "dp"), "tensor"),
        P(None, ("expert", "dp"), "tensor"),
    )
    out_specs = P(("expert", "dp"), "tensor")
    plan = stationary_plan if mesh.shape["expert"] == 4 and mesh.shape["tensor"] == 2 else gathered_plan
    return jax.shard_map(plan, mesh=mesh, in_specs=in_specs, out_specs=out_specs, check_vma=False)
```

```python
import functools

import jax
import jax.numpy as jnp
from jax import lax
from jax.experimental import pallas as pl
from jax.experimental.pallas import tpu as pltpu
from jax.sharding import PartitionSpec as P

BF = jnp.bfloat16
F32 = jnp.float32
VMEM_BYTES = 48 * 1024 * 1024


def gathered_plan(tokens, routes, gate_prob, token_count, gate_weight, up_weight, down_weight):
    experts = gate_weight.shape[0]
    stored_rows = gate_weight.shape[1]
    hidden_share = gate_weight.shape[2]
    tok_rows, top_slots = routes.shape
    capacity = min(tok_rows, tok_rows * top_slots * 5 // (4 * experts))
    expert_count = lax.axis_size("expert")
    replica_count = lax.axis_size("dp")
    model_width = stored_rows * expert_count * replica_count

    def relay(weight):
        arrived = lax.all_to_all(weight, "expert", split_axis=0, concat_axis=1, tiled=True)
        blocks = arrived.reshape(1, expert_count, 1, stored_rows, hidden_share)
        return lax.all_gather(blocks, "dp", axis=2, tiled=True).reshape(model_width, hidden_share)

    w_gate, w_up, w_down = relay(gate_weight), relay(up_weight), relay(down_weight)
    positions = jnp.arange(tok_rows)
    live_rows = positions < token_count[0]
    live_pair = jnp.repeat(live_rows, top_slots)
    route_flat = routes.reshape(-1)
    expert_ids = jnp.arange(experts)
    one_hot = ((route_flat[:, None] == expert_ids[None, :]) & live_pair[:, None]).astype(jnp.int32)
    pair_rank = jnp.sum((jnp.cumsum(one_hot, axis=0) - one_hot) * one_hot, axis=1)
    slot_of_pair = jnp.where(live_pair, route_flat * capacity + pair_rank, -1)
    slot_ids = jnp.arange(experts * capacity)
    assign_pair = (slot_ids[:, None] == slot_of_pair[None, :]).astype(BF)
    assign_slots = assign_pair.reshape(experts * capacity, tok_rows, top_slots)
    assign_bf16 = jnp.sum(assign_slots.astype(F32), axis=2).astype(BF)
    outgoing = jnp.dot(assign_bf16, tokens, preferred_element_type=F32).astype(BF)
    incoming = lax.all_to_all(
        outgoing.reshape(experts, capacity, tokens.shape[1]), "expert", split_axis=0, concat_axis=0, tiled=True
    )
    feature_piece = lax.all_gather(incoming, "tensor", axis=2, tiled=True)
    flat_piece = feature_piece.reshape(-1, feature_piece.shape[2])
    gate_proj = jnp.dot(flat_piece, w_gate, preferred_element_type=F32)
    up_proj = jnp.dot(flat_piece, w_up, preferred_element_type=F32)
    hidden = (jax.nn.silu(gate_proj) * up_proj).astype(BF)
    partial_value = lax.dot_general(hidden, w_down, (((1,), (1,)), ((), ())), preferred_element_type=F32)
    expert_out = lax.psum_scatter(partial_value.astype(BF), "tensor", scatter_dimension=1, tiled=True)
    returned = lax.all_to_all(
        expert_out.reshape(experts, capacity, -1), "expert", split_axis=0, concat_axis=0, tiled=True
    )
    returned_rows = returned.reshape(experts * capacity, -1)
    picked = jnp.einsum("cts,cd->std", assign_slots, returned_rows, preferred_element_type=F32)
    mixed = jnp.sum(gate_prob.T[:, :, None] * picked, axis=0)
    return mixed.astype(BF)


META_ROWS = 16
UNIT = 128


def split_in_three(value):
    high = value.astype(BF)
    rest = value - high.astype(F32)
    middle = rest.astype(BF)
    return high, middle, (rest - middle.astype(F32)).astype(BF)


def columns_of(token_refs, rows):
    held = jnp.concatenate([t[rows:, :rows].astype(F32).T for t in token_refs], axis=0)
    prob = [held[:, 2 + s : 3 + s] + held[:, 4 + s : 5 + s] + held[:, 6 + s : 7 + s] for s in range(2)]
    return held[:, 0:1], held[:, 1:2], prob[0], prob[1]


def send_order_kernel(where_ref, tokens_ref, route_ref, prob_ref, *out_refs):
    n_dp = len(out_refs)
    rows = tokens_ref.shape[0]
    width = tokens_ref.shape[1] // (2 * n_dp)
    core, z = where_ref[1], where_ref[2]
    meta = [route_ref[...].astype(BF), *split_in_three(prob_ref[...])]
    for k, out in enumerate(out_refs):
        target = lax.rem(z + k, n_dp)
        for j in range(2):
            slot = (lax.rem(core + j, 2) * n_dp + target) * width
            out[:rows, j * width : (j + 1) * width] = tokens_ref[:, pl.ds(pl.multiple_of(slot, width), width)]
        filler = jnp.zeros((META_ROWS - 8, rows), F32)
        block = jnp.concatenate([m.astype(F32) for m in meta] + [filler], axis=0).astype(BF)
        out[rows:, :] = jnp.zeros((META_ROWS, 2 * width), BF)
        out[rows:, :rows] = block


def place_kernel(where_ref, *refs):
    in_refs, out_ref = refs[:-1], refs[-1]
    n_dp = len(in_refs)
    width = out_ref.shape[1] // (2 * n_dp)
    core, z = where_ref[1], where_ref[2]
    for k, piece in enumerate(in_refs):
        source = lax.rem(z + k, n_dp)
        for j in range(2):
            slot = (lax.rem(core + j, 2) * n_dp + source) * width
            out_ref[:, pl.ds(pl.multiple_of(slot, width), width)] = piece[:, j * width : (j + 1) * width]


def gate_up_kernel(n, where_ref, *refs):
    own_refs, far_refs, out_refs = refs[:n], refs[n : 2 * n], refs[-n:]
    w_refs = refs[2 * n : -n]
    same = where_ref[3] == 1
    rows = own_refs[0].shape[0] - META_ROWS
    own = jnp.concatenate([r[:rows] for r in own_refs], axis=0)
    far = jnp.concatenate([r[:rows] for r in far_refs], axis=0)
    near_x = jnp.where(same, own, far)
    away_x = jnp.where(same, far, own)
    route = columns_of(own_refs, rows)[:2]
    for b in range(len(w_refs) // 6):
        gate, up, gate_core, up_core, far_w, far_core = w_refs[6 * b : 6 * b + 6]
        experts, width, unit = gate.shape
        slots = [None, None]
        for e in range(experts):
            mine = jnp.concatenate([gate[e], up[e]], axis=1)
            cores = jnp.concatenate([gate_core[e], up_core[e]], axis=1)
            part = jnp.dot(near_x[:, :width], mine, preferred_element_type=F32)
            part += jnp.dot(near_x[:, width:], cores, preferred_element_type=F32)
            part += jnp.dot(away_x[:, :width], far_w[e], preferred_element_type=F32)
            part += jnp.dot(away_x[:, width:], far_core[e], preferred_element_type=F32)
            for s in range(2):
                held = jnp.zeros_like(part) if e == 0 else slots[s]
                slots[s] = jnp.where(route[s] == float(e), part, held)
        for k, out in enumerate(out_refs):
            for s in range(2):
                out[s, :, 2 * b * unit : 2 * (b + 1) * unit] = slots[s][k * rows : (k + 1) * rows].astype(BF)


def hidden_kernel(n_spans, *refs):
    mine, got, out_ref = refs[:n_spans], refs[n_spans : 2 * n_spans], refs[-1]
    unit, at = UNIT, 0
    for a, b in zip(mine, got):
        for n in range(a.shape[-1] // (2 * unit)):
            gate_cols = slice(2 * n * unit, (2 * n + 1) * unit)
            up_cols = slice((2 * n + 1) * unit, (2 * n + 2) * unit)
            for s in range(2):
                gate = a[s, :, gate_cols].astype(F32) + b[s, :, gate_cols].astype(F32)
                up = a[s, :, up_cols].astype(F32) + b[s, :, up_cols].astype(F32)
                out_ref[s, :, at : at + unit] = (gate / (1.0 + jnp.exp(-gate)) * up).astype(BF)
            at += unit


def down_kernel(n, n_parts, first, where_ref, *refs):
    token_refs = refs[:n]
    h_refs = refs[n : n * (1 + n_parts)]
    w_refs = refs[n * (1 + n_parts) : n * (1 + n_parts) + 4]
    rest = refs[n * (1 + n_parts) + 4 :]
    same = where_ref[3] == 1
    rows = h_refs[0].shape[1]
    experts, width = w_refs[0].shape[0], w_refs[0].shape[1]
    route0, route1, prob0, prob1 = columns_of(token_refs, rows)
    hidden = [
        jnp.concatenate(
            [jnp.concatenate([h_refs[p * n + i][s] for p in range(n_parts)], axis=1) for i in range(n)], axis=0
        )
        for s in range(2)
    ]
    total = [None] * 4
    if not first:
        total = [jnp.concatenate([rest[i][:, j * width : (j + 1) * width] for i in range(n)], axis=0) for j in range(4)]
    for e in range(experts):
        one, two = route0 == float(e), route1 == float(e)
        h_e = jnp.where(one, hidden[0], jnp.where(two, hidden[1], jnp.zeros_like(hidden[1])))
        scale = jnp.where(one, prob0, jnp.where(two, prob1, 0.0))
        for j in range(4):
            term = scale * lax.dot_general(h_e, w_refs[j][e], (((1,), (1,)), ((), ())), preferred_element_type=F32)
            total[j] = term if total[j] is None else total[j] + term
    if first:
        for i in range(n):
            for j in range(4):
                rest[i][:, j * width : (j + 1) * width] = total[j][i * rows : (i + 1) * rows]
        return
    near_out, away_out = rest[n:]
    held = [t.astype(BF).reshape(n, rows, width) for t in total]
    for j in range(2):
        cols = slice(j * width, (j + 1) * width)
        near_out[:, :, cols] = jnp.where(same, held[j], held[j + 2])
        away_out[:, :, cols] = jnp.where(same, held[j + 2], held[j])


SMEM = pl.BlockSpec(memory_space=pltpu.SMEM)
WHOLE = pl.BlockSpec(memory_space=pltpu.VMEM)
PARAMS = pltpu.CompilerParams(vmem_limit_bytes=VMEM_BYTES)
LIGHT = pl.CostEstimate(flops=1, bytes_accessed=1, transcendentals=0)


def stationary_plan(tokens, routes, gate_prob, token_count, gate_weight, up_weight, down_weight):
    experts, width, share = gate_weight.shape
    rows = tokens.shape[0]
    n_dp = lax.axis_size("dp")
    place = lax.axis_index("expert")
    y, core, x, z = place // 2, place % 2, lax.axis_index("tensor"), lax.axis_index("dp")
    same = (x == y).astype(jnp.int32)
    where = jnp.stack([y, core, z, (x == y).astype(jnp.int32)]).astype(jnp.int32)

    def swap_y(v):
        return lax.ppermute(v, "expert", [(0, 2), (2, 0), (1, 3), (3, 1)])

    def swap_core(v):
        return lax.ppermute(v, "expert", [(0, 1), (1, 0), (2, 3), (3, 2)])

    def swap_x(v):
        return lax.ppermute(v, "tensor", [(0, 1), (1, 0)])

    def shift(v, k):
        return lax.ppermute(v, "dp", [(i, (i + k) % n_dp) for i in range(n_dp)])

    live = jnp.arange(rows)[None, :] < token_count[0]
    slots = jnp.where(live, routes.T, -1).astype(F32)

    send = pl.pallas_call(
        send_order_kernel,
        out_shape=[jax.ShapeDtypeStruct((rows + META_ROWS, 2 * width), BF)] * n_dp,
        in_specs=[SMEM] + [WHOLE] * 3,
        out_specs=[WHOLE] * n_dp,
        compiler_params=PARAMS,
        cost_estimate=LIGHT,
    )(where, tokens, slots, gate_prob.T)
    def cross_x(v, k):
        pairs = [(t * n_dp + i, (1 - t) * n_dp + (i + k) % n_dp) for t in range(2) for i in range(n_dp)]
        return lax.ppermute(v, ("tensor", "dp"), pairs)

    gate_core, up_core = swap_core(gate_weight), swap_core(up_weight)
    gate_core, up_core, *send = lax.optimization_barrier((gate_core, up_core, *send))
    own = [send[0]] + [shift(send[k], k) for k in range(1, n_dp)]
    stacked = swap_x(jnp.stack(own))
    far = [stacked[k] for k in range(n_dp)]

    blocks = share // UNIT

    def block(weights, n):
        return jnp.concatenate([w[:, :, n * UNIT : (n + 1) * UNIT] for w in weights], axis=2)

    def gate_up(units, over_y, over_y_core):
        def call(which):
            n = len(which)
            weights, w_specs = [], []
            for i in units:
                weights += [gate_weight, up_weight, gate_core, up_core]
                w_specs += [pl.BlockSpec((experts, width, UNIT), lambda _, i=i: (0, 0, i))] * 4
                for v in (over_y, over_y_core):
                    weights.append(v)
                    w_specs.append(pl.BlockSpec((None,) + v.shape[1:], lambda _, at=i - units[0]: (at, 0, 0, 0)))
            return pl.pallas_call(
                functools.partial(gate_up_kernel, n),
                grid=(1,),
                out_shape=[jax.ShapeDtypeStruct((2, rows, 2 * len(units) * UNIT), BF)] * n,
                in_specs=[SMEM] + [WHOLE] * (2 * n) + w_specs,
                out_specs=[WHOLE] * n,
                compiler_params=PARAMS,
                cost_estimate=LIGHT,
            )(where, *[own[k] for k in which], *[far[k] for k in which], *weights)

        (sent,) = call([1])
        kept = call([0] + list(range(2, n_dp)))
        return [kept[0], sent, *kept[1:]]

    def ring_step(parts, run, k):
        return (parts[k].astype(F32) + shift(run, 1).astype(F32)).astype(BF)

    def hidden_of(parts, gots):
        columns = sum(p[0].shape[2] for p in parts) // 2
        return pl.pallas_call(
            functools.partial(hidden_kernel, len(parts)),
            out_shape=jax.ShapeDtypeStruct((2, rows, columns), BF),
            in_specs=[WHOLE] * (2 * len(parts)),
            out_specs=WHOLE,
            compiler_params=PARAMS,
            cost_estimate=LIGHT,
        )(*[p[0] for p in parts], *gots)

    def ring_dp(v):
        held = [v]
        for _ in range(1, n_dp):
            held.append(shift(held[-1], 1))
        return held

    def gather_dp(v):
        return [v] + [shift(v, k) for k in range(1, n_dp)]

    bar = lax.optimization_barrier
    given = (gate_weight, up_weight)

    def pair(n):
        return jnp.stack([block(given, n), block(given, n + 1)])

    y01 = swap_y(pair(0))
    own, far, y01, *given = bar((own, far, y01, *given))

    yc01 = swap_core(y01)
    y23 = swap_y(pair(2))
    parts0 = gate_up([0, 1], y01, yc01)
    run0 = ring_step(parts0, parts0[1], 2)
    run0 = ring_step(parts0, run0, 3)
    down_core = swap_core(down_weight)
    y23, run0, down_core, *given = bar((y23, run0, down_core, *given))

    yc23 = swap_core(y23)
    y45 = swap_y(pair(4))
    got0 = shift(run0, 1)
    parts1 = gate_up([2, 3], y23, yc23)
    run1 = ring_step(parts1, parts1[1], 2)
    hidden0 = gather_dp(hidden_of([parts0], [got0]))
    run1 = ring_step(parts1, run1, 3)
    y45, run1, down_from, *hidden0 = bar((y45, run1, down_weight, *hidden0))

    yc45 = swap_core(y45)
    down_y = swap_y(down_from)
    got1 = shift(run1, 1)
    parts2 = gate_up([4, 5], y45, yc45)
    run2 = ring_step(parts2, parts2[1], 2)
    hidden1 = ring_dp(hidden_of([parts1], [got1]))
    run2 = ring_step(parts2, run2, 3)
    got2 = shift(run2, 1)
    got2, down_y, down_from, hidden1[2] = bar((got2, down_y, down_from, hidden1[2]))
    down_yc = swap_core(down_y)
    hidden2 = hidden_of([parts2], [got2])
    hidden2 = gather_dp(hidden2)
    hidden2[1], down_core, down_yc = bar((hidden2[1], down_core, down_yc))

    down_weights = (down_weight, down_core, down_y, down_yc)
    late = 2 * UNIT
    sums = pl.pallas_call(
        functools.partial(down_kernel, n_dp, 2, True),
        grid=(1,),
        out_shape=[jax.ShapeDtypeStruct((rows, 4 * width), F32)] * n_dp,
        in_specs=[SMEM]
        + [WHOLE] * (3 * n_dp)
        + [pl.BlockSpec((experts, width, share - late), lambda _: (0, 0, 0))] * 4,
        out_specs=[WHOLE] * n_dp,
        compiler_params=PARAMS,
        cost_estimate=pl.CostEstimate(flops=6_000_000_000, bytes_accessed=1, transcendentals=0),
    )(where, *own, *hidden0, *hidden1, *down_weights)

    hidden2[1], *sums = bar((hidden2[1], *sums))

    def down(which):
        n = len(which)
        last = pl.BlockSpec((experts, width, late), lambda _: (0, 0, share // late - 1))
        return pl.pallas_call(
            functools.partial(down_kernel, n, 1, False),
            grid=(1,),
            out_shape=[jax.ShapeDtypeStruct((n, rows, 2 * width), BF)] * 2,
            in_specs=[SMEM] + [WHOLE] * (2 * n) + [last] * 4 + [WHOLE] * n,
            out_specs=[WHOLE] * 2,
            compiler_params=PARAMS,
            cost_estimate=LIGHT,
        )(where, *[own[k] for k in which], *[hidden2[k] for k in which], *down_weights, *[sums[k] for k in which])

    back = [None] * n_dp
    order = list(range(2, n_dp)) + [1, 0]
    for which in (order[: n_dp // 2], order[n_dp // 2 :]):
        mine, other = down(which)
        total = (mine.astype(F32) + swap_x(other).astype(F32)).astype(BF)
        for i, k in enumerate(which):
            back[k] = total[i] if k == 0 else shift(total[i], -k)
    return pl.pallas_call(
        place_kernel,
        out_shape=jax.ShapeDtypeStruct(tokens.shape, BF),
        in_specs=[SMEM] + [WHOLE] * n_dp,
        out_specs=WHOLE,
        compiler_params=PARAMS,
        cost_estimate=LIGHT,
    )(where, *back)


def solution(mesh):
    in_specs = (
        P(("expert", "dp"), "tensor"),
        P(("expert", "dp"), None),
        P(("expert", "dp"), None),
        P(("expert", "dp")),
        P(None, ("expert", "dp"), "tensor"),
        P(None, ("expert", "dp"), "tensor"),
        P(None, ("expert", "dp"), "tensor"),
    )
    out_specs = P(("expert", "dp"), "tensor")
    plan = stationary_plan if mesh.shape["expert"] == 4 and mesh.shape["tensor"] == 2 else gathered_plan
    return jax.shard_map(plan, mesh=mesh, in_specs=in_specs, out_specs=out_specs, check_vma=False)
```

```python
import functools

import jax
import jax.numpy as jnp
from jax import lax
from jax.experimental import pallas as pl
from jax.experimental.pallas import tpu as pltpu
from jax.sharding import PartitionSpec as P

BF = jnp.bfloat16
F32 = jnp.float32
VMEM_BYTES = 48 * 1024 * 1024


def gathered_plan(tokens, routes, gate_prob, token_count, gate_weight, up_weight, down_weight):
    experts = gate_weight.shape[0]
    stored_rows = gate_weight.shape[1]
    hidden_share = gate_weight.shape[2]
    tok_rows, top_slots = routes.shape
    capacity = min(tok_rows, tok_rows * top_slots * 5 // (4 * experts))
    expert_count = lax.axis_size("expert")
    replica_count = lax.axis_size("dp")
    model_width = stored_rows * expert_count * replica_count

    def relay(weight):
        arrived = lax.all_to_all(weight, "expert", split_axis=0, concat_axis=1, tiled=True)
        blocks = arrived.reshape(1, expert_count, 1, stored_rows, hidden_share)
        return lax.all_gather(blocks, "dp", axis=2, tiled=True).reshape(model_width, hidden_share)

    w_gate, w_up, w_down = relay(gate_weight), relay(up_weight), relay(down_weight)
    positions = jnp.arange(tok_rows)
    live_rows = positions < token_count[0]
    live_pair = jnp.repeat(live_rows, top_slots)
    route_flat = routes.reshape(-1)
    expert_ids = jnp.arange(experts)
    one_hot = ((route_flat[:, None] == expert_ids[None, :]) & live_pair[:, None]).astype(jnp.int32)
    pair_rank = jnp.sum((jnp.cumsum(one_hot, axis=0) - one_hot) * one_hot, axis=1)
    slot_of_pair = jnp.where(live_pair, route_flat * capacity + pair_rank, -1)
    slot_ids = jnp.arange(experts * capacity)
    assign_pair = (slot_ids[:, None] == slot_of_pair[None, :]).astype(BF)
    assign_slots = assign_pair.reshape(experts * capacity, tok_rows, top_slots)
    assign_bf16 = jnp.sum(assign_slots.astype(F32), axis=2).astype(BF)
    outgoing = jnp.dot(assign_bf16, tokens, preferred_element_type=F32).astype(BF)
    incoming = lax.all_to_all(
        outgoing.reshape(experts, capacity, tokens.shape[1]), "expert", split_axis=0, concat_axis=0, tiled=True
    )
    feature_piece = lax.all_gather(incoming, "tensor", axis=2, tiled=True)
    flat_piece = feature_piece.reshape(-1, feature_piece.shape[2])
    gate_proj = jnp.dot(flat_piece, w_gate, preferred_element_type=F32)
    up_proj = jnp.dot(flat_piece, w_up, preferred_element_type=F32)
    hidden = (jax.nn.silu(gate_proj) * up_proj).astype(BF)
    partial_value = lax.dot_general(hidden, w_down, (((1,), (1,)), ((), ())), preferred_element_type=F32)
    expert_out = lax.psum_scatter(partial_value.astype(BF), "tensor", scatter_dimension=1, tiled=True)
    returned = lax.all_to_all(
        expert_out.reshape(experts, capacity, -1), "expert", split_axis=0, concat_axis=0, tiled=True
    )
    returned_rows = returned.reshape(experts * capacity, -1)
    picked = jnp.einsum("cts,cd->std", assign_slots, returned_rows, preferred_element_type=F32)
    mixed = jnp.sum(gate_prob.T[:, :, None] * picked, axis=0)
    return mixed.astype(BF)


META_ROWS = 16
UNIT = 128


def split_in_three(value):
    high = value.astype(BF)
    rest = value - high.astype(F32)
    middle = rest.astype(BF)
    return high, middle, (rest - middle.astype(F32)).astype(BF)


def columns_of(token_refs, rows):
    held = jnp.concatenate([t[rows:, :rows].astype(F32).T for t in token_refs], axis=0)
    prob = [held[:, 2 + s : 3 + s] + held[:, 4 + s : 5 + s] + held[:, 6 + s : 7 + s] for s in range(2)]
    return held[:, 0:1], held[:, 1:2], prob[0], prob[1]


def send_order_kernel(where_ref, tokens_ref, route_ref, prob_ref, *out_refs):
    n_dp = len(out_refs)
    rows = tokens_ref.shape[0]
    width = tokens_ref.shape[1] // (2 * n_dp)
    core, z = where_ref[1], where_ref[2]
    meta = [route_ref[...].astype(BF), *split_in_three(prob_ref[...])]
    for k, out in enumerate(out_refs):
        target = lax.rem(z + k, n_dp)
        for j in range(2):
            slot = (lax.rem(core + j, 2) * n_dp + target) * width
            out[:rows, j * width : (j + 1) * width] = tokens_ref[:, pl.ds(pl.multiple_of(slot, width), width)]
        filler = jnp.zeros((META_ROWS - 8, rows), F32)
        block = jnp.concatenate([m.astype(F32) for m in meta] + [filler], axis=0).astype(BF)
        out[rows:, :] = jnp.zeros((META_ROWS, 2 * width), BF)
        out[rows:, :rows] = block


def place_kernel(where_ref, *refs):
    in_refs, out_ref = refs[:-1], refs[-1]
    n_dp = len(in_refs)
    width = out_ref.shape[1] // (2 * n_dp)
    core, z = where_ref[1], where_ref[2]
    for k, piece in enumerate(in_refs):
        source = lax.rem(z + k, n_dp)
        for j in range(2):
            slot = (lax.rem(core + j, 2) * n_dp + source) * width
            out_ref[:, pl.ds(pl.multiple_of(slot, width), width)] = piece[:, j * width : (j + 1) * width]


def gate_up_kernel(n, where_ref, *refs):
    own_refs, far_refs, out_refs = refs[:n], refs[n : 2 * n], refs[-n:]
    w_refs = refs[2 * n : -n]
    same = where_ref[3] == 1
    rows = own_refs[0].shape[0] - META_ROWS
    own = jnp.concatenate([r[:rows] for r in own_refs], axis=0)
    far = jnp.concatenate([r[:rows] for r in far_refs], axis=0)
    near_x = jnp.where(same, own, far)
    away_x = jnp.where(same, far, own)
    route = columns_of(own_refs, rows)[:2]
    for b in range(len(w_refs) // 6):
        gate, up, gate_core, up_core, far_w, far_core = w_refs[6 * b : 6 * b + 6]
        experts, width, unit = gate.shape
        slots = [None, None]
        for e in range(experts):
            mine = jnp.concatenate([gate[e], up[e]], axis=1)
            cores = jnp.concatenate([gate_core[e], up_core[e]], axis=1)
            part = jnp.dot(near_x[:, :width], mine, preferred_element_type=F32)
            part += jnp.dot(near_x[:, width:], cores, preferred_element_type=F32)
            part += jnp.dot(away_x[:, :width], far_w[e], preferred_element_type=F32)
            part += jnp.dot(away_x[:, width:], far_core[e], preferred_element_type=F32)
            for s in range(2):
                held = jnp.zeros_like(part) if e == 0 else slots[s]
                slots[s] = jnp.where(route[s] == float(e), part, held)
        for k, out in enumerate(out_refs):
            for s in range(2):
                out[s, :, 2 * b * unit : 2 * (b + 1) * unit] = slots[s][k * rows : (k + 1) * rows].astype(BF)


def hidden_kernel(n_spans, *refs):
    mine, got, out_ref = refs[:n_spans], refs[n_spans : 2 * n_spans], refs[-1]
    unit, at = UNIT, 0
    for a, b in zip(mine, got):
        for n in range(a.shape[-1] // (2 * unit)):
            gate_cols = slice(2 * n * unit, (2 * n + 1) * unit)
            up_cols = slice((2 * n + 1) * unit, (2 * n + 2) * unit)
            for s in range(2):
                gate = a[s, :, gate_cols].astype(F32) + b[s, :, gate_cols].astype(F32)
                up = a[s, :, up_cols].astype(F32) + b[s, :, up_cols].astype(F32)
                out_ref[s, :, at : at + unit] = (gate / (1.0 + jnp.exp(-gate)) * up).astype(BF)
            at += unit


def down_kernel(n, n_parts, first, where_ref, *refs):
    token_refs = refs[:n]
    h_refs = refs[n : n * (1 + n_parts)]
    w_refs = refs[n * (1 + n_parts) : n * (1 + n_parts) + 4]
    rest = refs[n * (1 + n_parts) + 4 :]
    same = where_ref[3] == 1
    rows = h_refs[0].shape[1]
    experts, width = w_refs[0].shape[0], w_refs[0].shape[1]
    route0, route1, prob0, prob1 = columns_of(token_refs, rows)
    hidden = [
        jnp.concatenate(
            [jnp.concatenate([h_refs[p * n + i][s] for p in range(n_parts)], axis=1) for i in range(n)], axis=0
        )
        for s in range(2)
    ]
    total = [None] * 4
    if not first:
        total = [jnp.concatenate([rest[i][:, j * width : (j + 1) * width] for i in range(n)], axis=0) for j in range(4)]
    for e in range(experts):
        one, two = route0 == float(e), route1 == float(e)
        h_e = jnp.where(one, hidden[0], jnp.where(two, hidden[1], jnp.zeros_like(hidden[1])))
        scale = jnp.where(one, prob0, jnp.where(two, prob1, 0.0))
        for j in range(4):
            term = scale * lax.dot_general(h_e, w_refs[j][e], (((1,), (1,)), ((), ())), preferred_element_type=F32)
            total[j] = term if total[j] is None else total[j] + term
    if first:
        for i in range(n):
            for j in range(4):
                rest[i][:, j * width : (j + 1) * width] = total[j][i * rows : (i + 1) * rows]
        return
    near_out, away_out = rest[n:]
    held = [t.astype(BF).reshape(n, rows, width) for t in total]
    for j in range(2):
        cols = slice(j * width, (j + 1) * width)
        near_out[:, :, cols] = jnp.where(same, held[j], held[j + 2])
        away_out[:, :, cols] = jnp.where(same, held[j + 2], held[j])


SMEM = pl.BlockSpec(memory_space=pltpu.SMEM)
WHOLE = pl.BlockSpec(memory_space=pltpu.VMEM)
PARAMS = pltpu.CompilerParams(vmem_limit_bytes=VMEM_BYTES)
LIGHT = pl.CostEstimate(flops=1, bytes_accessed=1, transcendentals=0)


def stationary_plan(tokens, routes, gate_prob, token_count, gate_weight, up_weight, down_weight):
    experts, width, share = gate_weight.shape
    rows = tokens.shape[0]
    n_dp = lax.axis_size("dp")
    place = lax.axis_index("expert")
    y, core, x, z = place // 2, place % 2, lax.axis_index("tensor"), lax.axis_index("dp")
    same = (x == y).astype(jnp.int32)
    where = jnp.stack([y, core, z, (x == y).astype(jnp.int32)]).astype(jnp.int32)

    def swap_y(v):
        return lax.ppermute(v, "expert", [(0, 2), (2, 0), (1, 3), (3, 1)])

    def swap_core(v):
        return lax.ppermute(v, "expert", [(0, 1), (1, 0), (2, 3), (3, 2)])

    def swap_x(v):
        return lax.ppermute(v, "tensor", [(0, 1), (1, 0)])

    def shift(v, k):
        return lax.ppermute(v, "dp", [(i, (i + k) % n_dp) for i in range(n_dp)])

    live = jnp.arange(rows)[None, :] < token_count[0]
    slots = jnp.where(live, routes.T, -1).astype(F32)

    send = pl.pallas_call(
        send_order_kernel,
        out_shape=[jax.ShapeDtypeStruct((rows + META_ROWS, 2 * width), BF)] * n_dp,
        in_specs=[SMEM] + [WHOLE] * 3,
        out_specs=[WHOLE] * n_dp,
        compiler_params=PARAMS,
        cost_estimate=LIGHT,
    )(where, tokens, slots, gate_prob.T)
    gate_core, up_core = swap_core(gate_weight), swap_core(up_weight)
    gate_core, up_core, *send = lax.optimization_barrier((gate_core, up_core, *send))
    own = [send[0]] + [shift(send[k], k) for k in range(1, n_dp)]
    stacked = swap_x(jnp.stack([v[:rows] for v in own]))
    far = [stacked[k] for k in range(n_dp)]

    blocks = share // UNIT

    def block(weights, n):
        return jnp.concatenate([w[:, :, n * UNIT : (n + 1) * UNIT] for w in weights], axis=2)

    def gate_up(units, over_y, over_y_core):
        def call(which):
            n = len(which)
            weights, w_specs = [], []
            for i in units:
                weights += [gate_weight, up_weight, gate_core, up_core]
                w_specs += [pl.BlockSpec((experts, width, UNIT), lambda _, i=i: (0, 0, i))] * 4
                for v in (over_y, over_y_core):
                    weights.append(v)
                    w_specs.append(pl.BlockSpec((None,) + v.shape[1:], lambda _, at=i - units[0]: (at, 0, 0, 0)))
            return pl.pallas_call(
                functools.partial(gate_up_kernel, n),
                grid=(1,),
                out_shape=[jax.ShapeDtypeStruct((2, rows, 2 * len(units) * UNIT), BF)] * n,
                in_specs=[SMEM] + [WHOLE] * (2 * n) + w_specs,
                out_specs=[WHOLE] * n,
                compiler_params=PARAMS,
                cost_estimate=LIGHT,
            )(where, *[own[k] for k in which], *[far[k] for k in which], *weights)

        (sent,) = call([1])
        kept = call([0] + list(range(2, n_dp)))
        return [kept[0], sent, *kept[1:]]

    def ring_step(parts, run, k):
        return (parts[k].astype(F32) + shift(run, 1).astype(F32)).astype(BF)

    def hidden_of(parts, gots):
        columns = sum(p[0].shape[2] for p in parts) // 2
        return pl.pallas_call(
            functools.partial(hidden_kernel, len(parts)),
            out_shape=jax.ShapeDtypeStruct((2, rows, columns), BF),
            in_specs=[WHOLE] * (2 * len(parts)),
            out_specs=WHOLE,
            compiler_params=PARAMS,
            cost_estimate=LIGHT,
        )(*[p[0] for p in parts], *gots)

    def ring_dp(v):
        held = [v]
        for _ in range(1, n_dp):
            held.append(shift(held[-1], 1))
        return held

    def gather_dp(v):
        return [v] + [shift(v, k) for k in range(1, n_dp)]

    bar = lax.optimization_barrier
    given = (gate_weight, up_weight)

    def pair(n):
        return jnp.stack([block(given, n), block(given, n + 1)])

    y01 = swap_y(pair(0))
    own, far, y01, *given = bar((own, far, y01, *given))

    yc01 = swap_core(y01)
    y23 = swap_y(pair(2))
    parts0 = gate_up([0, 1], y01, yc01)
    run0 = ring_step(parts0, parts0[1], 2)
    run0 = ring_step(parts0, run0, 3)
    down_core = swap_core(down_weight)
    y23, run0, down_core, *given = bar((y23, run0, down_core, *given))

    yc23 = swap_core(y23)
    y45 = swap_y(pair(4))
    got0 = shift(run0, 1)
    parts1 = gate_up([2, 3], y23, yc23)
    run1 = ring_step(parts1, parts1[1], 2)
    hidden0 = gather_dp(hidden_of([parts0], [got0]))
    run1 = ring_step(parts1, run1, 3)
    y45, run1, down_from, *hidden0 = bar((y45, run1, down_weight, *hidden0))

    yc45 = swap_core(y45)
    down_y = swap_y(down_from)
    got1 = shift(run1, 1)
    parts2 = gate_up([4, 5], y45, yc45)
    run2 = ring_step(parts2, parts2[1], 2)
    hidden1 = ring_dp(hidden_of([parts1], [got1]))
    run2 = ring_step(parts2, run2, 3)
    got2 = shift(run2, 1)
    got2, down_y, down_from, hidden1[2] = bar((got2, down_y, down_from, hidden1[2]))
    down_yc = swap_core(down_y)
    hidden2 = hidden_of([parts2], [got2])
    hidden2 = gather_dp(hidden2)
    hidden2[1], down_yc = bar((hidden2[1], down_yc))

    down_weights = (down_weight, down_core, down_y, down_yc)
    late = 2 * UNIT
    sums = pl.pallas_call(
        functools.partial(down_kernel, n_dp, 2, True),
        grid=(1,),
        out_shape=[jax.ShapeDtypeStruct((rows, 4 * width), F32)] * n_dp,
        in_specs=[SMEM]
        + [WHOLE] * (3 * n_dp)
        + [pl.BlockSpec((experts, width, share - late), lambda _: (0, 0, 0))] * 4,
        out_specs=[WHOLE] * n_dp,
        compiler_params=PARAMS,
        cost_estimate=pl.CostEstimate(flops=6_000_000_000, bytes_accessed=1, transcendentals=0),
    )(where, *own, *hidden0, *hidden1, *down_weights)

    hidden2[1], *sums = bar((hidden2[1], *sums))

    def down(which):
        n = len(which)
        last = pl.BlockSpec((experts, width, late), lambda _: (0, 0, share // late - 1))
        return pl.pallas_call(
            functools.partial(down_kernel, n, 1, False),
            grid=(1,),
            out_shape=[jax.ShapeDtypeStruct((n, rows, 2 * width), BF)] * 2,
            in_specs=[SMEM] + [WHOLE] * (2 * n) + [last] * 4 + [WHOLE] * n,
            out_specs=[WHOLE] * 2,
            compiler_params=PARAMS,
            cost_estimate=LIGHT,
        )(where, *[own[k] for k in which], *[hidden2[k] for k in which], *down_weights, *[sums[k] for k in which])

    back = [None] * n_dp
    order = list(range(2, n_dp)) + [1, 0]
    for which in (order[: n_dp // 2], order[n_dp // 2 :]):
        mine, other = down(which)
        total = (mine.astype(F32) + swap_x(other).astype(F32)).astype(BF)
        for i, k in enumerate(which):
            back[k] = total[i] if k == 0 else shift(total[i], -k)
    return pl.pallas_call(
        place_kernel,
        out_shape=jax.ShapeDtypeStruct(tokens.shape, BF),
        in_specs=[SMEM] + [WHOLE] * n_dp,
        out_specs=WHOLE,
        compiler_params=PARAMS,
        cost_estimate=LIGHT,
    )(where, *back)


def solution(mesh):
    in_specs = (
        P(("expert", "dp"), "tensor"),
        P(("expert", "dp"), None),
        P(("expert", "dp"), None),
        P(("expert", "dp")),
        P(None, ("expert", "dp"), "tensor"),
        P(None, ("expert", "dp"), "tensor"),
        P(None, ("expert", "dp"), "tensor"),
    )
    out_specs = P(("expert", "dp"), "tensor")
    plan = stationary_plan if mesh.shape["expert"] == 4 and mesh.shape["tensor"] == 2 else gathered_plan
    return jax.shard_map(plan, mesh=mesh, in_specs=in_specs, out_specs=out_specs, check_vma=False)
```
